32 devices in a mesh: prow: 4 (over y, core), pcol: 8 (over z, x).
Axes of the slice: x: 2, y: 2, z: 4, core: 2. Of those that a mesh axis runs over, the one named last changes fastest.
Arguments:
- matrix: float32 [10240, 9216], P('prow', 'pcol'), as said below
- pivots: int32 [1024], replicated, may hold values from 0 to 10239, as said below
Outputs:
- updated: float32 [10240, 9216], P('prow', 'pcol')
The draws below stay inside these ranges and needn't reach their ends.
Inputs may be any that keep to these rules, and one draw needn't show every extreme that they name: For each i < 1024, pivots[i] is i or a row index of 1024 or more; indices of 1024 or more are distinct. `matrix`: the first 1024 columns hold the factored panel: below the diagonal, the multipliers of the lower factor.
All inputs are finite; a program needn't handle non-finite values.
Results may differ from the reference program's by a relative error of at most 0.000051.
Values sent between devices are 32-bit elements; how exact they have to be, the bound alone decides.
A program may use at most 128 MiB of HBM per device.

```python
import math
import jax
import jax.numpy as jnp
from jax import lax

NB = 1024
MR = 2560
EXTRA = 128
N_PROW = 4
N_PCOL = 8


def draw_matrix(key, part):
    rows_all = MR * N_PROW
    cols_all = (NB + EXTRA) * N_PCOL
    key_values = jax.random.fold_in(key, 21)
    column = lax.broadcasted_iota(jnp.int32, (rows_all, cols_all), 1)
    values_raw = jnp.clip(jax.random.normal(key_values, (rows_all, cols_all), jnp.float32), -6.0, 6.0)
    panel_scale = 0.6 / math.sqrt(NB)
    return jnp.where(column < NB, values_raw * panel_scale, values_raw).astype(jnp.float32)


def draw_pivots(key, part):
    total = MR * N_PROW
    key_rows = jax.random.fold_in(key, 11)
    key_keep = jax.random.fold_in(key, 12)
    shuffled = jax.random.permutation(key_rows, total - NB).astype(jnp.int32) + NB
    chosen = shuffled[:NB]
    position = jnp.arange(NB, dtype=jnp.int32)
    keeping = jax.random.randint(key_keep, (NB,), 0, 4) > 0
    keeping = keeping & (position != 0)
    kept_last = jnp.any((chosen == total - 1) & keeping)
    chosen = jnp.where(kept_last | (position != NB - 1), chosen, total - 1).astype(jnp.int32)
    keeping = keeping | (position == NB - 1) & jnp.logical_not(kept_last)
    return jnp.where(keeping, chosen, position).astype(jnp.int32)


def setup_inputs(seed: int = 0) -> dict:
    splits = jax.random.split(jax.random.key(seed), 3)
    matrix = draw_matrix(jax.random.fold_in(splits[2], 71), 0)
    pivots = draw_pivots(jax.random.fold_in(splits[2], 71), 0)
    return {"matrix": matrix, "pivots": pivots}


def reference(matrix, pivots):
    panel_width = pivots.shape[0]
    trailing = matrix[:, panel_width:]
    new_top = trailing[pivots]
    old_top = trailing[:panel_width]
    trailing = trailing.at[pivots].set(old_top)
    upper_rows = lax.linalg.triangular_solve(matrix[:panel_width, :panel_width], new_top, left_side=True, lower=True, unit_diagonal=True)
    below_rows = trailing[panel_width:] - jnp.dot(matrix[panel_width:, :panel_width].astype(jnp.float32), upper_rows.astype(jnp.float32), precision=lax.Precision.HIGHEST, preferred_element_type=jnp.float32)
    stacked = jnp.concatenate([upper_rows, below_rows], axis=0)
    return jnp.concatenate([matrix[:, :panel_width], stacked], axis=1)
```

```python
import functools
import jax
import jax.numpy as jnp
from jax import lax
from jax.experimental import pallas as pl
from jax.experimental.pallas import tpu as pltpu
from jax.sharding import PartitionSpec as P

MESH = pl.DeviceIdType.MESH
CHUNK = 32
BLOCK = 128
F32 = jnp.float32
BF16 = jnp.bfloat16


def exact_dot(a, b):
    return jnp.dot(a, b, precision=lax.Precision.HIGHEST, preferred_element_type=F32)


def plain_dot(a, b):
    return jnp.dot(a, b, preferred_element_type=F32)


def loop(low, high, body, **options):
    def step(i, carry):
        body(i)
        return carry

    lax.fori_loop(low, high, step, 0, **options)


def unit_lower_inverse(block):
    size = block.shape[0]
    row = lax.broadcasted_iota(jnp.int32, (size, size), 0)
    col = lax.broadcasted_iota(jnp.int32, (size, size), 1)
    inverse = jnp.where(row == col, 1.0, 0.0).astype(F32)
    level = 0
    while (1 << level) < size:
        same = (row >> (level + 1)) == (col >> (level + 1))
        below = (((row >> level) & 1) == 1) & (((col >> level) & 1) == 0)
        middle = jnp.where(same & below, block, 0.0)
        if level == 0:
            inverse = inverse - middle
        else:
            inverse = inverse - exact_dot(exact_dot(inverse, middle), inverse)
        level += 1
    return inverse


def kernel(
    nx, nz, ny, pivot_smem, pivot_row, matrix, out,
    mat, panel, new_top, slots, old_top, part0, part1, factor,
    load_sem, a_recv, b_recv, a_send, b_send, row_send, row_recv, top_send, top_recv,
    ld_send, ld_recv, half_send, half_recv, ring_send, ring_recv, store_sem, free_sem,
):
    rows, cols = mat.shape
    width = factor.shape[0]
    half = width // 2
    steps = rows // CHUNK // 2
    head = steps // 5
    ld_steps = width // CHUNK // 2
    prow, pcol = lax.axis_index("prow"), lax.axis_index("pcol")
    y, core = prow // 2, prow % 2
    z, x = pcol // nx, pcol % nx
    source = pcol == 0
    partner = y * 2 + (1 - core)
    y_next = lax.rem(y + 1, ny) * 2 + core
    y_prev = lax.rem(y + ny - 1, ny) * 2 + core

    barrier = pltpu.get_barrier_semaphore()
    has_left, has_right, has_down, has_up = x > 0, x < nx - 1, z > 0, z < nz - 1

    def greet(p, q):
        pl.semaphore_signal(barrier, inc=1, device_id=(p, q), device_id_type=MESH)

    for has, q in ((has_left, pcol - 1), (has_right, pcol + 1), (has_down, pcol - nx), (has_up, pcol + nx)):
        pl.when(has)(functools.partial(greet, prow, q))
    greet(partner, pcol)
    greet(y_next, pcol)
    if ny > 2:
        greet(y_prev, pcol)

    mat_load = pltpu.make_async_copy(matrix, mat, load_sem.at[0])
    mat_load.start()
    panel_load = pltpu.make_async_copy(matrix.at[:, pl.ds(0, width)], panel, load_sem.at[1])
    pl.when(source)(panel_load.start)
    top_load = pltpu.make_async_copy(matrix.at[pl.ds(0, width), :], old_top, load_sem.at[2])
    pl.when(prow == 0)(top_load.start)

    count = sum(h.astype(jnp.int32) for h in (has_left, has_right, has_down, has_up)) + (3 if ny > 2 else 2)
    pl.semaphore_wait(barrier, count)

    def chunk_rows(c, which):
        if which == 0:
            k = jnp.where(c < head, ld_steps * 2 + c, jnp.where(c < head + ld_steps, c - head, c + ld_steps))
        else:
            k = jnp.where(
                c < head, steps + ld_steps + c, jnp.where(c < head + ld_steps, c - head + ld_steps, c + steps)
            )
        return pl.ds(pl.multiple_of(k * CHUNK, CHUNK), CHUNK)

    def copy_to(which, c, way, q):
        recv, send = ((a_recv, a_send), (b_recv, b_send))[which]
        piece = panel.at[chunk_rows(c, which)]
        return pltpu.make_async_remote_copy(
            piece, piece, send.at[way, c], recv.at[c], device_id=(prow, q), device_id_type=MESH
        )

    ways = (
        (
            ((z == 0) & (x < nx - 1), pcol + 1),
            ((x >= 1) & (z < nz - 1), pcol + nx),
            ((x == 1) & (z >= 1), pcol - 1),
        ),
        (
            ((x == 0) & (z < nz - 1), pcol + nx),
            ((z >= 1) & (x < nx - 1), pcol + 1),
            ((z == 1) & (x >= 1), pcol - nx),
        ),
    )

    def forward(c):
        for which in (0, 1):
            pl.when(jnp.logical_not(source))(lambda: copy_to(which, c, 0, pcol).wait_recv())
            for way, (go, q) in enumerate(ways[which]):
                pl.when(go)(lambda: copy_to(which, c, way, q).start())

    def ld_copy(which, c, way, p):
        piece = chunk_rows(c, which)
        slot = which * ld_steps + c - head
        return pltpu.make_async_remote_copy(
            panel.at[piece], factor.at[piece], ld_send.at[way, slot], ld_recv.at[slot],
            device_id=(p, pcol), device_id_type=MESH,
        )

    def spread_factor(c):
        @pl.when(prow == 0)
        def _():
            for which in (0, 1):
                ld_copy(which, c, 0, 1).start()
                ld_copy(which, c, 1, 2).start()

    @pl.when(source)
    def _():
        panel_load.wait()
        loop(0, head, forward)

        @pl.when(prow == 0)
        def _():
            def invert(k):
                begin = pl.multiple_of(k * BLOCK, BLOCK)
                place = (pl.ds(begin, BLOCK), pl.ds(begin, BLOCK))
                panel[place] = unit_lower_inverse(panel[place])

            loop(0, width // BLOCK, invert)

        loop(head, steps, forward)

    top_copy = pltpu.make_async_remote_copy(
        matrix.at[pl.ds(0, width), :], old_top, top_send.at[0], top_recv.at[0],
        device_id=(1, pcol), device_id_type=MESH,
    )
    pl.when(prow == 0)(top_copy.start)
    mat_load.wait()

    def relay(c):
        pl.when(jnp.logical_not(source))(lambda: forward(c))

    per_step = width // head

    def gather_step(c):
        relay(c)

        def one(j):
            i = c * per_step + j
            pivot = pivot_smem[i]
            owner = lax.div(pivot, rows)
            keep = (owner == prow) | ((prow == 0) & (owner >= 2))
            local = jnp.where(owner == prow, pivot - owner * rows, i)
            row = mat[pl.ds(local, 1), :]
            new_top[pl.ds(i, 1), :] = jnp.where(keep, row, 0.0)

        loop(0, per_step, one, unroll=8)

    loop(0, head, gather_step)

    my_half = pl.ds(pl.multiple_of(core * half, half), half)
    other_half = pl.ds(pl.multiple_of((1 - core) * half, half), half)
    half_copy = pltpu.make_async_remote_copy(
        new_top.at[other_half], slots.at[0], half_send.at[0], half_recv.at[0],
        device_id=(partner, pcol), device_id_type=MESH,
    )
    half_copy.start()

    def factor_step(c):
        relay(c)
        spread_factor(c)

    loop(head, head + 2, factor_step)
    half_copy.wait()
    pl.semaphore_signal(free_sem, inc=1, device_id=(partner, pcol), device_id_type=MESH)
    new_top[my_half, :] = new_top[my_half, :] + slots[0]

    def ring_copy(s):
        return pltpu.make_async_remote_copy(
            new_top.at[my_half] if s == 0 else slots.at[s], slots.at[s + 1], ring_send.at[s], ring_recv.at[s],
            device_id=(y_next, pcol), device_id_type=MESH,
        )

    ring_copy(0).start()
    loop(head + 2, head + ld_steps, factor_step)
    after = head + ld_steps
    loop(after, after + 5, relay)

    pivot_col = jnp.transpose(pivot_row[...])[:, 0:1]
    for s in range(ny - 1):
        ring_copy(s).wait_recv()
        if s < ny - 2:
            ring_copy(s + 1).start()
    ring_copy(0).wait_send()

    def combine(h):
        place = pl.ds(h * half, half)
        pivot = pivot_col[h * half:(h + 1) * half]

        def owned(chip):
            return (pivot >= chip * 2 * rows) & (pivot < (chip + 1) * 2 * rows)

        total = jnp.where(owned(y), new_top[place, :], 0.0)
        for s in range(ny - 1):
            origin = lax.rem(y + ny - 1 - s, ny)
            total = jnp.where(owned(origin), slots[s + 1], total)
        new_top[place, :] = total

        @pl.when(y > 0)
        def _():
            for s in range(ny - 1):
                @pl.when(y == s + 1)
                def _():
                    old_top[place, :] = slots[s + 1]

    for h in (0, 1):
        pl.when(core == h)(functools.partial(combine, h))

    new_copy = pltpu.make_async_remote_copy(
        new_top.at[my_half], new_top.at[my_half], half_send.at[1], half_recv.at[1],
        device_id=(partner, pcol), device_id_type=MESH,
    )
    pl.semaphore_wait(free_sem, 1)
    new_copy.start()
    old_copy = pltpu.make_async_remote_copy(
        old_top.at[my_half], old_top.at[my_half], half_send.at[2], half_recv.at[2],
        device_id=(partner, pcol), device_id_type=MESH,
    )
    pl.when(y > 0)(old_copy.start)

    loop(after + 5, after + 8, relay)

    pl.when(y > 0)(old_copy.wait_recv)
    pl.when(prow == 1)(top_copy.wait_recv)
    pl.when(prow == 0)(top_load.wait)

    def split_old(k):
        place = pl.ds(pl.multiple_of(k * BLOCK, BLOCK), BLOCK)
        value = old_top[place, :]
        high = value.astype(BF16)
        part0[place, :] = high
        part1[place, :] = (value - high.astype(F32)).astype(BF16)

    loop(0, width // BLOCK, split_old)

    tile = 256
    tiles = rows // tile
    trailing = (pcol * cols + lax.broadcasted_iota(jnp.int32, (1, cols), 1)) >= width

    def exchange(t):
        place = pl.ds(pl.multiple_of(t * tile, tile), tile)
        ident = prow * rows + t * tile + lax.broadcasted_iota(jnp.int32, (tile, width), 0)
        hit = (pivot_row[0:1, :] == ident) & (ident >= width)
        pick = jnp.where(hit, 1.0, 0.0)
        hits = jnp.sum(pick, axis=1, keepdims=True)
        pick = pick.astype(BF16)
        moved = plain_dot(pick, part0[...]) + plain_dot(pick, part1[...])
        mat[place, :] = jnp.where((hits > 0.5) & trailing, moved, mat[place, :])

    rest_steps = steps - after - 8

    def exchange_step(c):
        relay(c)
        exchange(c - after - 8)

    loop(after + 8, steps, exchange_step)
    loop(rest_steps, tiles, exchange)

    @pl.when(prow > 0)
    def _():
        for slot in range(2 * ld_steps):
            which, c = slot // ld_steps, head + slot % ld_steps
            ld_copy(which, c, 0, prow).wait_recv()

    def relay_chunks(way, p, act):
        def one(slot):
            piece = pl.ds(pl.multiple_of(slot * CHUNK, CHUNK), CHUNK)
            act(pltpu.make_async_remote_copy(
                factor.at[piece], factor.at[piece], ld_send.at[way, slot], ld_recv.at[slot],
                device_id=(p, pcol), device_id_type=MESH,
            ))

        loop(0, 2 * ld_steps, one)

    even = (prow >= 2) & (core == 0)
    pl.when(even)(lambda: relay_chunks(0, prow + 1, lambda d: d.start()))
    onward = even & (y < ny - 1)
    if ny > 2:
        pl.when(onward)(lambda: relay_chunks(1, prow + 2, lambda d: d.start()))

    @pl.when(prow == 0)
    def _():
        local = pltpu.make_async_copy(panel.at[pl.ds(0, width)], factor, load_sem.at[3])
        local.start()
        local.wait()

    new_copy.wait()

    for k in range(width // BLOCK):
        place = pl.ds(k * BLOCK, BLOCK)
        right = new_top[place, :]
        if k:
            right = right - exact_dot(factor[place, pl.ds(0, k * BLOCK)], new_top[pl.ds(0, k * BLOCK), :])
        solved = exact_dot(factor[place, pl.ds(k * BLOCK, BLOCK)], right)
        new_top[place, :] = solved
        high = solved.astype(BF16)
        part0[place, :] = high
        part1[place, :] = (solved - high.astype(F32)).astype(BF16)

    def store(t):
        place = pl.ds(pl.multiple_of(t * tile, tile), tile)
        return pltpu.make_async_copy(mat.at[place], out.at[place], store_sem.at[t])

    def update(t):
        place = pl.ds(pl.multiple_of(t * tile, tile), tile)
        value = panel[place, :]
        high = value.astype(BF16)
        low = (value - high.astype(F32)).astype(BF16)
        product = plain_dot(high, part0[...]) + (plain_dot(high, part1[...]) + plain_dot(low, part0[...]))
        old = mat[place, :]
        mat[place, :] = jnp.where(trailing, old - product, old)
        store(t).start()

    top_tiles = width // tile

    def put_top(t):
        place = pl.ds(pl.multiple_of(t * tile, tile), tile)
        mat[place, :] = jnp.where(trailing, new_top[place, :], mat[place, :])
        store(t).start()

    pl.when(prow == 0)(lambda: loop(0, top_tiles, put_top))
    pl.when(prow > 0)(lambda: loop(0, top_tiles, update))
    loop(top_tiles, tiles, update)
    loop(0, tiles, lambda t: store(t).wait())

    def drain(c):
        for which in (0, 1):
            for way, (go, q) in enumerate(ways[which]):
                pl.when(go)(lambda: copy_to(which, c, way, q).wait_send())

    loop(0, steps, drain)

    @pl.when(prow == 0)
    def _():
        def one(c):
            for which in (0, 1):
                ld_copy(which, c, 0, 1).wait_send()
                ld_copy(which, c, 1, 2).wait_send()

        loop(head, head + ld_steps, one)
        top_copy.wait_send()

    pl.when(even)(lambda: relay_chunks(0, prow + 1, lambda d: d.wait_send()))
    if ny > 2:
        pl.when(onward)(lambda: relay_chunks(1, prow + 2, lambda d: d.wait_send()))
    pl.when(y > 0)(old_copy.wait_send)
    for s in range(1, ny - 1):
        ring_copy(s).wait_send()


def on_device(nx, nz, ny, matrix, pivots):
    rows, cols = matrix.shape
    width = pivots.shape[0]
    steps = rows // CHUNK // 2
    chunks = width // CHUNK
    dma = pltpu.SemaphoreType.DMA
    pivot_row = jnp.broadcast_to(pivots[None, :], (8, width))
    return pl.pallas_call(
        functools.partial(kernel, nx, nz, ny),
        out_shape=jax.ShapeDtypeStruct((rows, cols), F32),
        in_specs=[
            pl.BlockSpec(memory_space=pltpu.SMEM),
            pl.BlockSpec(memory_space=pltpu.VMEM),
            pl.BlockSpec(memory_space=pl.ANY),
        ],
        out_specs=pl.BlockSpec(memory_space=pl.ANY),
        scratch_shapes=[
            pltpu.VMEM((rows, cols), F32),
            pltpu.VMEM((rows, width), F32),
            pltpu.VMEM((width, cols), F32),
            pltpu.VMEM((ny, width // 2, cols), F32),
            pltpu.VMEM((width, cols), F32),
            pltpu.VMEM((width, cols), BF16),
            pltpu.VMEM((width, cols), BF16),
            pltpu.VMEM((width, width), F32),
            dma((4,)),
            dma((steps,)),
            dma((steps,)),
            dma((3, steps)),
            dma((3, steps)),
            dma((1,)),
            dma((1,)),
            dma((1,)),
            dma((1,)),
            dma((2, chunks)),
            dma((chunks,)),
            dma((3,)),
            dma((3,)),
            dma((ny - 1,)),
            dma((ny - 1,)),
            dma((rows // 256,)),
            pltpu.SemaphoreType.REGULAR,
        ],
        compiler_params=pltpu.CompilerParams(
            collective_id=0, has_side_effects=True, vmem_limit_bytes=62 * 1024 * 1024
        ),
    )(pivots, pivot_row, matrix)


def solution(mesh):
    ny = mesh.shape["prow"] // 2
    nz = 4
    nx = mesh.shape["pcol"] // nz
    return jax.shard_map(
        functools.partial(on_device, nx, nz, ny),
        mesh=mesh,
        in_specs=(P("prow", "pcol"), P()),
        out_specs=P("prow", "pcol"),
        check_vma=False,
    )
```

```python
import functools
import jax
import jax.numpy as jnp
from jax import lax
from jax.experimental import pallas as pl
from jax.experimental.pallas import tpu as pltpu
from jax.sharding import PartitionSpec as P

MESH = pl.DeviceIdType.MESH
CHUNK = 32
BLOCK = 128
F32 = jnp.float32
BF16 = jnp.bfloat16


def exact_dot(a, b):
    return jnp.dot(a, b, precision=lax.Precision.HIGHEST, preferred_element_type=F32)


def plain_dot(a, b):
    return jnp.dot(a, b, preferred_element_type=F32)


def loop(low, high, body, **options):
    def step(i, carry):
        body(i)
        return carry

    lax.fori_loop(low, high, step, 0, **options)


def unit_lower_inverse(block):
    size = block.shape[0]
    row = lax.broadcasted_iota(jnp.int32, (size, size), 0)
    col = lax.broadcasted_iota(jnp.int32, (size, size), 1)
    inverse = jnp.where(row == col, 1.0, 0.0).astype(F32)
    level = 0
    while (1 << level) < size:
        same = (row >> (level + 1)) == (col >> (level + 1))
        below = (((row >> level) & 1) == 1) & (((col >> level) & 1) == 0)
        middle = jnp.where(same & below, block, 0.0)
        if level == 0:
            inverse = inverse - middle
        else:
            inverse = inverse - exact_dot(exact_dot(inverse, middle), inverse)
        level += 1
    return inverse


def kernel(
    nx, nz, ny, pivot_smem, pivot_row, matrix, out,
    mat, panel, new_top, slots, old_top, part0, part1, factor,
    load_sem, a_recv, b_recv, a_send, b_send, row_send, row_recv, top_send, top_recv,
    ld_send, ld_recv, half_send, half_recv, ring_send, ring_recv, store_sem, free_sem,
):
    rows, cols = mat.shape
    width = factor.shape[0]
    half = width // 2
    steps = rows // CHUNK // 2
    head = steps // 5
    ld_steps = width // CHUNK // 2
    prow, pcol = lax.axis_index("prow"), lax.axis_index("pcol")
    y, core = prow // 2, prow % 2
    z, x = pcol // nx, pcol % nx
    source = pcol == 0
    partner = y * 2 + (1 - core)
    y_next = lax.rem(y + 1, ny) * 2 + core
    y_prev = lax.rem(y + ny - 1, ny) * 2 + core

    barrier = pltpu.get_barrier_semaphore()
    has_left, has_right, has_down, has_up = x > 0, x < nx - 1, z > 0, z < nz - 1

    def greet(p, q):
        pl.semaphore_signal(barrier, inc=1, device_id=(p, q), device_id_type=MESH)

    for has, q in ((has_left, pcol - 1), (has_right, pcol + 1), (has_down, pcol - nx), (has_up, pcol + nx)):
        pl.when(has)(functools.partial(greet, prow, q))
    greet(partner, pcol)
    greet(y_next, pcol)
    if ny > 2:
        greet(y_prev, pcol)

    mat_load = pltpu.make_async_copy(matrix, mat, load_sem.at[0])
    mat_load.start()
    panel_load = pltpu.make_async_copy(matrix.at[:, pl.ds(0, width)], panel, load_sem.at[1])
    pl.when(source)(panel_load.start)
    top_load = pltpu.make_async_copy(matrix.at[pl.ds(0, width), :], old_top, load_sem.at[2])
    pl.when(prow == 0)(top_load.start)

    count = sum(h.astype(jnp.int32) for h in (has_left, has_right, has_down, has_up)) + (3 if ny > 2 else 2)
    pl.semaphore_wait(barrier, count)

    def chunk_rows(c, which):
        if which == 0:
            k = jnp.where(c < head, ld_steps * 2 + c, jnp.where(c < head + ld_steps, c - head, c + ld_steps))
        else:
            k = jnp.where(
                c < head, steps + ld_steps + c, jnp.where(c < head + ld_steps, c - head + ld_steps, c + steps)
            )
        return pl.ds(pl.multiple_of(k * CHUNK, CHUNK), CHUNK)

    def copy_to(which, c, way, q):
        recv, send = ((a_recv, a_send), (b_recv, b_send))[which]
        piece = panel.at[chunk_rows(c, which)]
        return pltpu.make_async_remote_copy(
            piece, piece, send.at[way, c], recv.at[c], device_id=(prow, q), device_id_type=MESH
        )

    ways = (
        (
            ((z == 0) & (x < nx - 1), pcol + 1),
            ((x >= 1) & (z < nz - 1), pcol + nx),
            ((x == 1) & (z >= 1), pcol - 1),
        ),
        (
            ((x == 0) & (z < nz - 1), pcol + nx),
            ((z >= 1) & (x < nx - 1), pcol + 1),
            ((z == 1) & (x >= 1), pcol - nx),
        ),
    )

    def ld_copy(which, c, way, p):
        piece = chunk_rows(c, which)
        slot = which * ld_steps + c - head
        return pltpu.make_async_remote_copy(
            panel.at[piece], factor.at[piece], ld_send.at[way, slot], ld_recv.at[slot],
            device_id=(p, pcol), device_id_type=MESH,
        )

    def forward(which, c):
        for way, (go, q) in enumerate(ways[which]):
            pl.when(go)(lambda: copy_to(which, c, way, q).start())

        @pl.when((prow == 0) & (c >= head) & (c < head + ld_steps))
        def _():
            ld_copy(which, c, 0, 1).start()
            ld_copy(which, c, 1, 2).start()

    def send_both(c):
        forward(0, c)
        forward(1, c)

    depths = (
        jnp.where(z == 0, x, jnp.where(x == 0, z + 2, z + x)),
        jnp.where(x == 0, z, jnp.where(z == 0, x + 2, z + x)),
    )
    all_steps = steps + 2 * max(nx + nz - 2, nx + 1, nz + 1)

    def relay(step):
        for which in (0, 1):
            c = step - 2 * depths[which]

            @pl.when(jnp.logical_not(source) & (c >= 0) & (c < steps))
            def _():
                copy_to(which, c, 0, pcol).wait_recv()
                forward(which, c)

    @pl.when(source)
    def _():
        panel_load.wait()
        loop(0, head, send_both)

        @pl.when(prow == 0)
        def _():
            def invert(k):
                begin = pl.multiple_of(k * BLOCK, BLOCK)
                place = (pl.ds(begin, BLOCK), pl.ds(begin, BLOCK))
                panel[place] = unit_lower_inverse(panel[place])

            loop(0, width // BLOCK, invert)

        loop(head, steps, send_both)

    top_copy = pltpu.make_async_remote_copy(
        matrix.at[pl.ds(0, width), :], old_top, top_send.at[0], top_recv.at[0],
        device_id=(1, pcol), device_id_type=MESH,
    )
    pl.when(prow == 0)(top_copy.start)
    mat_load.wait()

    per_step = width // head

    def gather_step(c):
        relay(c)

        def one(j):
            i = c * per_step + j
            pivot = pivot_smem[i]
            owner = lax.div(pivot, rows)
            keep = (owner == prow) | ((prow == 0) & (owner >= 2))
            local = jnp.where(owner == prow, pivot - owner * rows, i)
            row = mat[pl.ds(local, 1), :]
            new_top[pl.ds(i, 1), :] = jnp.where(keep, row, 0.0)

        loop(0, per_step, one, unroll=8)

    loop(0, head, gather_step)

    my_half = pl.ds(pl.multiple_of(core * half, half), half)
    other_half = pl.ds(pl.multiple_of((1 - core) * half, half), half)
    half_copy = pltpu.make_async_remote_copy(
        new_top.at[other_half], slots.at[0], half_send.at[0], half_recv.at[0],
        device_id=(partner, pcol), device_id_type=MESH,
    )
    half_copy.start()

    loop(head, head + 2, relay)
    half_copy.wait()
    pl.semaphore_signal(free_sem, inc=1, device_id=(partner, pcol), device_id_type=MESH)
    new_top[my_half, :] = new_top[my_half, :] + slots[0]

    def ring_copy(s):
        return pltpu.make_async_remote_copy(
            new_top.at[my_half] if s == 0 else slots.at[s], slots.at[s + 1], ring_send.at[s], ring_recv.at[s],
            device_id=(y_next, pcol), device_id_type=MESH,
        )

    ring_copy(0).start()
    loop(head + 2, head + ld_steps, relay)
    after = head + ld_steps
    loop(after, after + 5, relay)

    pivot_col = jnp.transpose(pivot_row[...])[:, 0:1]
    for s in range(ny - 1):
        ring_copy(s).wait_recv()
        if s < ny - 2:
            ring_copy(s + 1).start()
    ring_copy(0).wait_send()

    def combine(h):
        place = pl.ds(h * half, half)
        pivot = pivot_col[h * half:(h + 1) * half]

        def owned(chip):
            return (pivot >= chip * 2 * rows) & (pivot < (chip + 1) * 2 * rows)

        total = jnp.where(owned(y), new_top[place, :], 0.0)
        for s in range(ny - 1):
            origin = lax.rem(y + ny - 1 - s, ny)
            total = jnp.where(owned(origin), slots[s + 1], total)
        new_top[place, :] = total

        @pl.when(y > 0)
        def _():
            for s in range(ny - 1):
                @pl.when(y == s + 1)
                def _():
                    old_top[place, :] = slots[s + 1]

    for h in (0, 1):
        pl.when(core == h)(functools.partial(combine, h))

    new_copy = pltpu.make_async_remote_copy(
        new_top.at[my_half], new_top.at[my_half], half_send.at[1], half_recv.at[1],
        device_id=(partner, pcol), device_id_type=MESH,
    )
    pl.semaphore_wait(free_sem, 1)
    new_copy.start()
    old_copy = pltpu.make_async_remote_copy(
        old_top.at[my_half], old_top.at[my_half], half_send.at[2], half_recv.at[2],
        device_id=(partner, pcol), device_id_type=MESH,
    )
    pl.when(y > 0)(old_copy.start)

    loop(after + 5, after + 8, relay)

    pl.when(y > 0)(old_copy.wait_recv)
    pl.when(prow == 1)(top_copy.wait_recv)
    pl.when(prow == 0)(top_load.wait)

    def split_old(k):
        place = pl.ds(pl.multiple_of(k * BLOCK, BLOCK), BLOCK)
        value = old_top[place, :]
        high = value.astype(BF16)
        part0[place, :] = high
        part1[place, :] = (value - high.astype(F32)).astype(BF16)

    loop(0, width // BLOCK, split_old)

    tile = 256
    tiles = rows // tile
    trailing = (pcol * cols + lax.broadcasted_iota(jnp.int32, (1, cols), 1)) >= width

    def exchange(t):
        place = pl.ds(pl.multiple_of(t * tile, tile), tile)
        ident = prow * rows + t * tile + lax.broadcasted_iota(jnp.int32, (tile, width), 0)
        hit = (pivot_row[0:1, :] == ident) & (ident >= width)
        pick = jnp.where(hit, 1.0, 0.0)
        hits = jnp.sum(pick, axis=1, keepdims=True)
        pick = pick.astype(BF16)
        moved = plain_dot(pick, part0[...]) + plain_dot(pick, part1[...])
        mat[place, :] = jnp.where((hits > 0.5) & trailing, moved, mat[place, :])

    def exchange_step(c):
        relay(c)
        exchange(c - after - 8)

    loop(after + 8, after + 8 + tiles, exchange_step)
    loop(after + 8 + tiles, all_steps, relay)

    @pl.when(prow > 0)
    def _():
        for slot in range(2 * ld_steps):
            which, c = slot // ld_steps, head + slot % ld_steps
            ld_copy(which, c, 0, prow).wait_recv()

    def relay_chunks(way, p, act):
        def one(slot):
            piece = pl.ds(pl.multiple_of(slot * CHUNK, CHUNK), CHUNK)
            act(pltpu.make_async_remote_copy(
                factor.at[piece], factor.at[piece], ld_send.at[way, slot], ld_recv.at[slot],
                device_id=(p, pcol), device_id_type=MESH,
            ))

        loop(0, 2 * ld_steps, one)

    even = (prow >= 2) & (core == 0)
    pl.when(even)(lambda: relay_chunks(0, prow + 1, lambda d: d.start()))
    onward = even & (y < ny - 1)
    if ny > 2:
        pl.when(onward)(lambda: relay_chunks(1, prow + 2, lambda d: d.start()))

    @pl.when(prow == 0)
    def _():
        local = pltpu.make_async_copy(panel.at[pl.ds(0, width)], factor, load_sem.at[3])
        local.start()
        local.wait()

    new_copy.wait()

    for k in range(width // BLOCK):
        place = pl.ds(k * BLOCK, BLOCK)
        right = new_top[place, :]
        if k:
            right = right - exact_dot(factor[place, pl.ds(0, k * BLOCK)], new_top[pl.ds(0, k * BLOCK), :])
        solved = exact_dot(factor[place, pl.ds(k * BLOCK, BLOCK)], right)
        new_top[place, :] = solved
        high = solved.astype(BF16)
        part0[place, :] = high
        part1[place, :] = (solved - high.astype(F32)).astype(BF16)

    def store(t):
        place = pl.ds(pl.multiple_of(t * tile, tile), tile)
        return pltpu.make_async_copy(mat.at[place], out.at[place], store_sem.at[t])

    def update(t):
        place = pl.ds(pl.multiple_of(t * tile, tile), tile)
        value = panel[place, :]
        high = value.astype(BF16)
        low = (value - high.astype(F32)).astype(BF16)
        product = plain_dot(high, part0[...]) + (plain_dot(high, part1[...]) + plain_dot(low, part0[...]))
        old = mat[place, :]
        mat[place, :] = jnp.where(trailing, old - product, old)
        store(t).start()

    top_tiles = width // tile

    def put_top(t):
        place = pl.ds(pl.multiple_of(t * tile, tile), tile)
        mat[place, :] = jnp.where(trailing, new_top[place, :], mat[place, :])
        store(t).start()

    pl.when(prow == 0)(lambda: loop(0, top_tiles, put_top))
    pl.when(prow > 0)(lambda: loop(0, top_tiles, update))
    loop(top_tiles, tiles, update)
    loop(0, tiles, lambda t: store(t).wait())

    def drain(c):
        for which in (0, 1):
            for way, (go, q) in enumerate(ways[which]):
                pl.when(go)(lambda: copy_to(which, c, way, q).wait_send())

    loop(0, steps, drain)

    @pl.when(prow == 0)
    def _():
        def one(c):
            for which in (0, 1):
                ld_copy(which, c, 0, 1).wait_send()
                ld_copy(which, c, 1, 2).wait_send()

        loop(head, head + ld_steps, one)
        top_copy.wait_send()

    pl.when(even)(lambda: relay_chunks(0, prow + 1, lambda d: d.wait_send()))
    if ny > 2:
        pl.when(onward)(lambda: relay_chunks(1, prow + 2, lambda d: d.wait_send()))
    pl.when(y > 0)(old_copy.wait_send)
    for s in range(1, ny - 1):
        ring_copy(s).wait_send()


def on_device(nx, nz, ny, matrix, pivots):
    rows, cols = matrix.shape
    width = pivots.shape[0]
    steps = rows // CHUNK // 2
    chunks = width // CHUNK
    dma = pltpu.SemaphoreType.DMA
    pivot_row = jnp.broadcast_to(pivots[None, :], (8, width))
    return pl.pallas_call(
        functools.partial(kernel, nx, nz, ny),
        out_shape=jax.ShapeDtypeStruct((rows, cols), F32),
        in_specs=[
            pl.BlockSpec(memory_space=pltpu.SMEM),
            pl.BlockSpec(memory_space=pltpu.VMEM),
            pl.BlockSpec(memory_space=pl.ANY),
        ],
        out_specs=pl.BlockSpec(memory_space=pl.ANY),
        scratch_shapes=[
            pltpu.VMEM((rows, cols), F32),
            pltpu.VMEM((rows, width), F32),
            pltpu.VMEM((width, cols), F32),
            pltpu.VMEM((ny, width // 2, cols), F32),
            pltpu.VMEM((width, cols), F32),
            pltpu.VMEM((width, cols), BF16),
            pltpu.VMEM((width, cols), BF16),
            pltpu.VMEM((width, width), F32),
            dma((4,)),
            dma((steps,)),
            dma((steps,)),
            dma((3, steps)),
            dma((3, steps)),
            dma((1,)),
            dma((1,)),
            dma((1,)),
            dma((1,)),
            dma((2, chunks)),
            dma((chunks,)),
            dma((3,)),
            dma((3,)),
            dma((ny - 1,)),
            dma((ny - 1,)),
            dma((rows // 256,)),
            pltpu.SemaphoreType.REGULAR,
        ],
        compiler_params=pltpu.CompilerParams(
            collective_id=0, has_side_effects=True, vmem_limit_bytes=62 * 1024 * 1024
        ),
    )(pivots, pivot_row, matrix)


def solution(mesh):
    ny = mesh.shape["prow"] // 2
    nz = 4
    nx = mesh.shape["pcol"] // nz
    return jax.shard_map(
        functools.partial(on_device, nx, nz, ny),
        mesh=mesh,
        in_specs=(P("prow", "pcol"), P()),
        out_specs=P("prow", "pcol"),
        check_vma=False,
    )
```
